512 devices in a mesh: ctx: 64 (over y, x, z_hi), img: 8 (over z_lo, core).
Axes of the slice: x: 4, y: 4, z: 16 (z_hi: 4, z_lo: 4; z = z_hi * 4 + z_lo), core: 2. Of those that a mesh axis runs over, the one named last changes fastest.
Arguments:
- self_query_rows: bfloat16 [8192, 8192], P('ctx', 'img'), may hold values from -128 to 128
- text_key_value: bfloat16 [8192, 2, 1024], P('ctx', None, 'img'), may hold values from -16 to 16
- cross_query_rows: bfloat16 [8192, 8192], P('ctx', 'img'), may hold values from -128 to 128
- vision_key_value: bfloat16 [64, 64, 2, 1024], P('ctx', 'img'), may hold values from -16 to 16
- doc_start: int32 [128], P('ctx'), may hold values from 0 to 8128, as said below
- image_mask: int32 [128, 64], P('ctx'), may hold values from 0 to 1, as said below
Outputs:
- self_out: bfloat16 [8192, 8192], P('ctx', 'img')
- cross_out: bfloat16 [8192, 8192], P('ctx', 'img')
The draws below stay inside these ranges and needn't reach their ends.
Inputs may be any that keep to these rules, and one draw needn't show every extreme that they name: Documents are runs of whole mask blocks: doc_start[b] is a multiple of 64, at most b * 64, never falls from one block to the next, and is 0 for the first block. `image_mask`: 1 where the text of mask block b may attend image i; every block may attend at least one image.
All inputs are finite; a program needn't handle non-finite values.
Results may differ from the reference program's by a relative error of at most 0.0049.
Values may be sent and summed in bfloat16 or wider, within the bound.
No kernel may reach another device: no remote copies, remote signals or barrier semaphores. Data moves between devices by JAX's collectives and lax.ppermute only.
A program may use at most 64 MiB of HBM per device.

```python
import math
import jax
import jax.numpy as jnp
from jax import lax

QUERY_HEADS = 64
KEY_VALUE_HEADS = 8
HEAD_WIDTH = 128
VISION_TOKENS = 64
MBLK = 64
TEXT_TOKENS = 8192
PAGE_IMAGES = 64
BLOCKS = 128


def mixed_normal(key, shape):
    key_one = jax.random.fold_in(key, 0)
    gaussian = jnp.clip(jax.random.normal(key_one, shape, jnp.float32), -6.0, 6.0)
    return gaussian


def row_scales(key, shape, lowest, highest):
    return jnp.exp(jax.random.uniform(key, shape, jnp.float32, math.log(lowest), math.log(highest)))


def text_fields(key, repeat_count):
    key = jax.random.fold_in(key, 101)
    subkeys = jax.random.split(key, 4)
    column_span = KEY_VALUE_HEADS * HEAD_WIDTH
    marked = (jnp.arange(TEXT_TOKENS) % 61 == 7)[:, None]
    scales = row_scales(subkeys[0], (TEXT_TOKENS, 1), 0.3, 3.0)
    scales = jnp.where(marked & (repeat_count > 0), 1.5, scales)
    keyset = mixed_normal(subkeys[1], (TEXT_TOKENS, column_span)) * scales
    before = jnp.roll(marked, -1, axis=0)
    keyset = jnp.where(before & (repeat_count > 0), 0.994 * jnp.roll(keyset, -1, axis=0), keyset)
    valueset = mixed_normal(subkeys[2], (TEXT_TOKENS, column_span)) * row_scales(subkeys[3], (TEXT_TOKENS, 1), 1.0 / 3.0, 3.0)
    return (jnp.clip(keyset, -16.0, 16.0), jnp.clip(valueset, -16.0, 16.0))


def vision_fields(key, repeat_count):
    key = jax.random.fold_in(key, 202)
    subkeys = jax.random.split(key, 4)
    column_span = KEY_VALUE_HEADS * HEAD_WIDTH
    marked = (jnp.arange(VISION_TOKENS) % 53 == 9)[None, :, None]
    scales = row_scales(subkeys[0], (PAGE_IMAGES, VISION_TOKENS, 1), 0.3, 3.0)
    scales = jnp.where(marked & (repeat_count > 0), 1.5, scales)
    keyset = mixed_normal(subkeys[1], (PAGE_IMAGES, VISION_TOKENS, column_span)) * scales
    before = jnp.roll(marked, -1, axis=1)
    keyset = jnp.where(before & (repeat_count > 0), 0.994 * jnp.roll(keyset, -1, axis=1), keyset)
    valueset = mixed_normal(subkeys[2], (PAGE_IMAGES, VISION_TOKENS, column_span)) * row_scales(subkeys[3], (PAGE_IMAGES, VISION_TOKENS, 1), 1.0 / 3.0, 3.0)
    return (jnp.clip(keyset, -16.0, 16.0), jnp.clip(valueset, -16.0, 16.0))


def draw_text_key_value(key, part):
    keyset, valueset = text_fields(key, 0.0)
    return jnp.stack([keyset, valueset], axis=1).astype(jnp.bfloat16)


def draw_vision_key_value(key, part):
    keyset, valueset = vision_fields(key, 0.0)
    return jnp.stack([keyset, valueset], axis=2).astype(jnp.bfloat16)


def draw_self_query_rows(key, part):
    own_key = jax.random.fold_in(key, 3)
    return mixed_normal(own_key, (TEXT_TOKENS, QUERY_HEADS * HEAD_WIDTH)).astype(jnp.bfloat16)


def draw_cross_query_rows(key, part):
    own_key = jax.random.fold_in(key, 4)
    return mixed_normal(own_key, (TEXT_TOKENS, QUERY_HEADS * HEAD_WIDTH)).astype(jnp.bfloat16)


def draw_doc_start(key, part):
    key = jax.random.fold_in(key, 7)
    key_roll, key_place = jax.random.split(key)
    block_ids = jnp.arange(BLOCKS, dtype=jnp.int32)
    rolled = jax.random.randint(key_roll, (BLOCKS,), 0, 8)
    placed = jax.random.randint(key_place, (), BLOCKS // 2, BLOCKS)
    breaks = (rolled == 0) & (block_ids >= 3 * BLOCKS // 4) | (block_ids == 0) | (block_ids == placed)
    starts = jnp.where(breaks, block_ids * MBLK, 0).astype(jnp.int32)
    return lax.cummax(starts, axis=0)


def draw_image_mask(key, part):
    key = jax.random.fold_in(key, 5)
    key_level, key_pick = jax.random.split(key)
    level = jax.random.randint(key_level, (BLOCKS, 1), 1, 9)
    picked = jax.random.randint(key_pick, (BLOCKS, PAGE_IMAGES), 0, 8)
    owner = jnp.arange(BLOCKS, dtype=jnp.int32) * PAGE_IMAGES // BLOCKS
    forced = jnp.arange(PAGE_IMAGES, dtype=jnp.int32)[None, :] == owner[:, None]
    return ((picked < level) | forced).astype(jnp.int32)


def setup_inputs(seed: int = 0) -> dict:
    streams_of = jax.random.split(jax.random.key(seed), 7)
    self_query_rows = draw_self_query_rows(jax.random.fold_in(streams_of[6], 71), 0)
    text_key_value = draw_text_key_value(jax.random.fold_in(streams_of[6], 71), 0)
    cross_query_rows = draw_cross_query_rows(jax.random.fold_in(streams_of[6], 71), 0)
    vision_key_value = draw_vision_key_value(jax.random.fold_in(streams_of[6], 71), 0)
    doc_start = draw_doc_start(jax.random.fold_in(streams_of[6], 71), 0)
    image_mask = draw_image_mask(jax.random.fold_in(streams_of[6], 71), 0)
    return dict(self_query_rows=self_query_rows, text_key_value=text_key_value, cross_query_rows=cross_query_rows, vision_key_value=vision_key_value, doc_start=doc_start, image_mask=image_mask)


NEGATIVE = -1e30


def softmax_rows(queries, key_rows, value_rows, allowed, factor):
    scores = jnp.einsum("qgd,sd->qgs", queries.astype(jnp.float32), key_rows.astype(jnp.float32)) * factor
    visible = allowed[:, None, :]
    scores = jnp.where(visible, scores, NEGATIVE)
    top_score = jnp.max(scores, axis=-1, keepdims=True)
    weights = jnp.where(visible, jnp.exp(scores - top_score), 0.0)
    totals = jnp.sum(weights, axis=-1)
    rounded = lax.optimization_barrier(weights.astype(jnp.bfloat16)).astype(jnp.float32)
    mixed = jnp.einsum("qgs,sd->qgd", rounded, value_rows.astype(jnp.float32))
    return mixed / totals[..., None]


def reference(self_query_rows, text_key_value, cross_query_rows, vision_key_value, doc_start, image_mask):
    group_width = QUERY_HEADS // KEY_VALUE_HEADS
    factor = HEAD_WIDTH ** -0.5
    block_rows = math.gcd(TEXT_TOKENS, 512)
    block_count = TEXT_TOKENS // block_rows
    text_key_rows = text_key_value[:, 0].reshape(TEXT_TOKENS, KEY_VALUE_HEADS, HEAD_WIDTH).transpose(1, 0, 2)
    text_value_rows = text_key_value[:, 1].reshape(TEXT_TOKENS, KEY_VALUE_HEADS, HEAD_WIDTH).transpose(1, 0, 2)
    vision_key_rows = vision_key_value[:, :, 0].reshape(PAGE_IMAGES * VISION_TOKENS, KEY_VALUE_HEADS, HEAD_WIDTH).transpose(1, 0, 2)
    vision_value_rows = vision_key_value[:, :, 1].reshape(PAGE_IMAGES * VISION_TOKENS, KEY_VALUE_HEADS, HEAD_WIDTH).transpose(1, 0, 2)
    token_start = jnp.repeat(doc_start, MBLK)
    token_mask = jnp.repeat(image_mask, MBLK, axis=0) > 0
    key_pos = jnp.arange(TEXT_TOKENS, dtype=jnp.int32)
    key_image = jnp.arange(PAGE_IMAGES * VISION_TOKENS, dtype=jnp.int32) // VISION_TOKENS
    self_head_count = self_query_rows.reshape(TEXT_TOKENS, KEY_VALUE_HEADS, group_width, HEAD_WIDTH)
    cross_head_count = cross_query_rows.reshape(TEXT_TOKENS, KEY_VALUE_HEADS, group_width, HEAD_WIDTH)

    def one_block(block_index):
        row_start = (block_index * block_rows).astype(jnp.int32)
        positions = row_start + jnp.arange(block_rows, dtype=jnp.int32)
        starts = lax.dynamic_slice_in_dim(token_start, row_start, block_rows, 0)
        self_allowed = (key_pos[None, :] <= positions[:, None]) & (key_pos[None, :] >= starts[:, None])
        mask_rows = lax.dynamic_slice_in_dim(token_mask, row_start, block_rows, 0)
        cross_allowed = mask_rows[:, key_image]
        self_rows = lax.dynamic_slice_in_dim(self_head_count, row_start, block_rows, 0).transpose(1, 0, 2, 3)
        cross_rows = lax.dynamic_slice_in_dim(cross_head_count, row_start, block_rows, 0).transpose(1, 0, 2, 3)
        self_mixed = lax.map(lambda inputs: softmax_rows(inputs[0], inputs[1], inputs[2], self_allowed, factor), (self_rows, text_key_rows, text_value_rows))
        cross_mixed = lax.map(lambda inputs: softmax_rows(inputs[0], inputs[1], inputs[2], cross_allowed, factor), (cross_rows, vision_key_rows, vision_value_rows))
        self_block = self_mixed.transpose(1, 0, 2, 3).reshape(block_rows, QUERY_HEADS * HEAD_WIDTH).astype(jnp.bfloat16)
        cross_block = cross_mixed.transpose(1, 0, 2, 3).reshape(block_rows, QUERY_HEADS * HEAD_WIDTH).astype(jnp.bfloat16)
        return self_block, cross_block

    self_all, cross_all = lax.map(one_block, jnp.arange(block_count, dtype=jnp.int32))
    return self_all.reshape(TEXT_TOKENS, QUERY_HEADS * HEAD_WIDTH), cross_all.reshape(TEXT_TOKENS, QUERY_HEADS * HEAD_WIDTH)
```

```python
import functools

import jax
import jax.numpy as jnp
from jax import lax
from jax.experimental import pallas as pl
from jax.experimental.pallas import tpu as pltpu
from jax.sharding import PartitionSpec as P

QUERY_HEADS = 64
KEY_VALUE_HEADS = 8
GROUP = QUERY_HEADS // KEY_VALUE_HEADS
HEAD_WIDTH = 128
MBLK = 64
VISION_TOKENS = 64
NEGATIVE = -1e30
SCALE = HEAD_WIDTH**-0.5 * 1.4426950408889634

SIDE = 4
ROWS = 128
PIECE = 2 * ROWS + 2 * VISION_TOKENS
SELF_CHUNKS = 4
CROSS_IMAGES = 8
SELF_ROWS = 256
CROSS_ROWS = 256


def flat(y, x, z, img):
    return ((y * SIDE + x) * SIDE + z) * 8 + img


def all_places():
    return [
        (y, x, z, img)
        for y in range(SIDE)
        for x in range(SIDE)
        for z in range(SIDE)
        for img in range(8)
    ]


def swap_pairs():
    pairs = []
    for y, x, z, img in all_places():
        core = img % 2
        if core != y // 2:
            pairs.append((flat(y, x, z, img), flat(3 - y, x, z, img ^ 1)))
        else:
            pairs.append((flat(y, x, z, img), flat(y, x, z, img)))
    return pairs


def vision_groups():
    return [
        [flat(yy, x, z, img) for yy in (y, 3 - y) for img in range(8)]
        for y in (0, 1)
        for x in range(SIDE)
        for z in range(SIDE)
    ]


def z_groups():
    return [
        [flat(y, x, z, img) for z in range(SIDE)]
        for y in range(SIDE)
        for x in range(SIDE)
        for img in range(8)
    ]


def plane_groups():
    groups = []
    for half in (0, 1):
        for z in range(SIDE):
            for img in range(8):
                core = img % 2
                held = (0, 1) if core == 0 else (2, 3)
                chips = [h if core == half else 3 - h for h in held]
                groups.append([flat(y, x, z, img) for y in chips for x in range(SIDE)])
    return groups


def step(q, keys, values, m_ref, l_ref, acc_ref, rows, visible):
    scores = lax.dot_general(
        q, keys, (((1,), (1,)), ((), ())), preferred_element_type=jnp.float32
    )
    if visible is not None:
        scores = jnp.where(visible, scores, NEGATIVE)
    old = m_ref[rows, :]
    new = jnp.maximum(old, jnp.max(scores, axis=1, keepdims=True))
    weights = jnp.exp2((scores - new[:, :1]) * SCALE)
    if visible is not None:
        weights = jnp.where(visible, weights, 0.0)
    shrink = jnp.exp2((old - new) * SCALE)
    m_ref[rows, :] = new
    l_ref[rows, :] = l_ref[rows, :] * shrink + jnp.sum(weights, axis=1, keepdims=True)
    acc_ref[rows, :] = acc_ref[rows, :] * shrink + jnp.dot(
        weights.astype(jnp.bfloat16), values, preferred_element_type=jnp.float32
    )


def kernel(
    meta, qs_ref, qc_ref, own_ref, other_ref, os_ref, oc_ref, kv, q_ref, m_ref, l_ref, acc_ref, images, sems
):
    row_chunk = meta[1, 2]
    core = row_chunk // 32
    copies = [
        pltpu.make_async_copy(ref, kv.at[pl.ds(32 * (core if i == 0 else 1 - core), 32)], sems.at[i])
        for i, ref in enumerate((own_ref, other_ref))
    ]
    for copy in copies:
        copy.start()

    def reset():
        m_ref[...] = jnp.full_like(m_ref, NEGATIVE)
        l_ref[...] = jnp.zeros_like(l_ref)
        acc_ref[...] = jnp.zeros_like(acc_ref)

    for b in range(2):
        for g in range(GROUP):
            q_ref[b * 512 + g * 64 : b * 512 + g * 64 + 64, :] = qc_ref[
                b * 64 : b * 64 + 64, g * 128 : g * 128 + 128
            ]
    reset()
    counts = []
    for b in range(2):

        def gather(i, count, b=b):
            images[b, count] = i
            return count + meta[0, b * 64 + i]

        counts.append(lax.fori_loop(0, 64, gather, 0, unroll=8))
    for copy in copies:
        copy.wait()
    for b in range(2):
        count = counts[b]
        width = CROSS_IMAGES * VISION_TOKENS

        def block(t, masked, b=b, count=count):
            picks = [
                images[b, jnp.minimum(t * CROSS_IMAGES + u, count - 1)] for u in range(CROSS_IMAGES)
            ]
            keys = jnp.concatenate(
                [kv[i, 2 * ROWS : 2 * ROWS + VISION_TOKENS, :] for i in picks], axis=0
            )
            values = jnp.concatenate(
                [kv[i, 2 * ROWS + VISION_TOKENS : PIECE, :] for i in picks], axis=0
            )
            visible = None
            if masked:
                spot = lax.broadcasted_iota(jnp.int32, (CROSS_ROWS, width), 1)
                visible = spot < (count - t * CROSS_IMAGES) * VISION_TOKENS
            for r in range(0, 512, CROSS_ROWS):
                rows = pl.ds(b * 512 + r, CROSS_ROWS)
                step(q_ref[rows, :], keys, values, m_ref, l_ref, acc_ref, rows, visible)

        full = count // CROSS_IMAGES

        @pl.loop(0, full)
        def _(t, block=block):
            block(t, False)

        @pl.when(full * CROSS_IMAGES < count)
        def _(block=block, full=full):
            block(full, True)

    for b in range(2):
        for g in range(GROUP):
            rows = slice(b * 512 + g * 64, b * 512 + g * 64 + 64)
            oc_ref[b * 64 : b * 64 + 64, g * 128 : g * 128 + 128] = (
                acc_ref[rows, :] / l_ref[rows, :]
            ).astype(jnp.bfloat16)

    for g in range(GROUP):
        q_ref[g * 128 : g * 128 + 128, :] = qs_ref[:, g * 128 : g * 128 + 128]
    reset()
    start0 = meta[1, 0] * MBLK
    start1 = meta[1, 1] * MBLK
    width = SELF_CHUNKS * ROWS
    first = start0 // width
    last = row_chunk // SELF_CHUNKS
    clear = (start1 + width - 1) // width

    def text(t, masked):
        piece = kv[pl.ds(t * SELF_CHUNKS, SELF_CHUNKS), 0 : 2 * ROWS, :]
        keys = piece[:, :ROWS].reshape(width, HEAD_WIDTH)
        values = piece[:, ROWS:].reshape(width, HEAD_WIDTH)
        visible = None
        if masked:
            spot = t * width + lax.broadcasted_iota(jnp.int32, (SELF_ROWS, width), 1)
            row = lax.broadcasted_iota(jnp.int32, (SELF_ROWS, width), 0) % ROWS
            start = jnp.where(row < MBLK, start0, start1)
            visible = (spot <= row_chunk * ROWS + row) & (spot >= start)
        for r in range(0, GROUP * ROWS, SELF_ROWS):
            rows = pl.ds(r, SELF_ROWS)
            step(q_ref[rows, :], keys, values, m_ref, l_ref, acc_ref, rows, visible)

    @pl.loop(first, last + 1)
    def _(t):
        masked = (t == last) | (t < clear)

        @pl.when(masked)
        def _():
            text(t, True)

        @pl.when(jnp.logical_not(masked))
        def _():
            text(t, False)

    for g in range(GROUP):
        rows = slice(g * 128, g * 128 + 128)
        os_ref[:, g * 128 : g * 128 + 128] = (acc_ref[rows, :] / l_ref[rows, :]).astype(jnp.bfloat16)


def attend(meta, self_q, cross_q, own, other):
    whole = pl.BlockSpec(memory_space=pltpu.VMEM)
    anywhere = pl.BlockSpec(memory_space=pl.ANY)
    out = jax.ShapeDtypeStruct((ROWS, GROUP * HEAD_WIDTH), jnp.bfloat16)
    state = pltpu.VMEM((GROUP * ROWS, 128), jnp.float32)
    return pl.pallas_call(
        kernel,
        out_shape=(out, out),
        in_specs=[pl.BlockSpec(memory_space=pltpu.SMEM), whole, whole, anywhere, anywhere],
        out_specs=(whole, whole),
        scratch_shapes=[
            pltpu.VMEM((64, PIECE, HEAD_WIDTH), jnp.bfloat16),
            pltpu.VMEM((GROUP * ROWS, HEAD_WIDTH), jnp.bfloat16),
            state,
            state,
            state,
            pltpu.SMEM((2, 128), jnp.int32),
            pltpu.SemaphoreType.DMA((2,)),
        ],
        compiler_params=pltpu.CompilerParams(vmem_limit_bytes=40 * 1024 * 1024),
        name="attend",
    )(meta, self_q, cross_q, own, other)


AXES = ("ctx", "img")


def body(self_q, text, cross_q, vision, doc_start, image_mask):
    core = lax.axis_index("img") % 2
    swap = functools.partial(lax.ppermute, axis_name=AXES, perm=swap_pairs())

    with jax.named_scope("text_swap"):
        numbers = jnp.concatenate([doc_start // MBLK, lax.axis_index("ctx")[None]])
        meta = jnp.stack([image_mask.reshape(128), jnp.pad(numbers, (0, 125))])
        meta = jnp.pad(meta.astype(jnp.bfloat16), ((0, 14), (0, 0)))
        text = jnp.concatenate([text[:, 0], text[:, 1], meta], axis=0)
        text = swap(text)
        meta = text[2 * ROWS : 2 * ROWS + 2].astype(jnp.int32)

    with jax.named_scope("vision_heads"):
        heads = vision.reshape(8, 2, 4, 2, HEAD_WIDTH).transpose(3, 2, 1, 0, 4)
        heads = jnp.broadcast_to(heads[:, :, None], (2, 4, 2, 2, 8, HEAD_WIDTH))
        heads = lax.all_to_all(
            heads.reshape(16, 16, HEAD_WIDTH), AXES, 0, 0, axis_index_groups=vision_groups(), tiled=True
        )
        heads = lax.dynamic_slice_in_dim(heads, core * 8, 8, 0)
        heads = heads.reshape(8, 2, 8, HEAD_WIDTH).transpose(1, 0, 2, 3).reshape(128, HEAD_WIDTH)

    with jax.named_scope("query_swap"):
        cross_q = swap(cross_q)
        self_q = swap(self_q)

    with jax.named_scope("along_z"):
        piece = jnp.concatenate([text[: 2 * ROWS], heads], axis=0)
        piece = jnp.broadcast_to(piece[None], (4, PIECE, HEAD_WIDTH))
        piece = lax.all_to_all(piece, AXES, 0, 0, axis_index_groups=z_groups(), tiled=True)

    with jax.named_scope("half_plane"):
        piece = jnp.broadcast_to(piece[None], (8, 4, PIECE, HEAD_WIDTH))
        piece = lax.all_to_all(piece, AXES, 0, 0, axis_index_groups=plane_groups(), tiled=True)
        own = piece.reshape(32, PIECE, HEAD_WIDTH)

    with jax.named_scope("cores"):
        other = lax.ppermute(own, "img", [(i, i ^ 1) for i in range(8)])

    with jax.named_scope("attention"):
        self_out, cross_out = attend(meta, self_q, cross_q, own, other)

    with jax.named_scope("return_rows"):
        return swap(self_out), swap(cross_out)


def solution(mesh):
    placed = (
        P("ctx", "img"),
        P("ctx", None, "img"),
        P("ctx", "img"),
        P("ctx", "img", None, None),
        P("ctx"),
        P("ctx", None),
    )
    return jax.shard_map(
        body,
        mesh=mesh,
        in_specs=placed,
        out_specs=(P("ctx", "img"), P("ctx", "img")),
        check_vma=False,
    )
```

```python
import functools

import jax
import jax.numpy as jnp
from jax import lax
from jax.experimental import pallas as pl
from jax.experimental.pallas import tpu as pltpu
from jax.sharding import PartitionSpec as P

QUERY_HEADS = 64
KEY_VALUE_HEADS = 8
GROUP = QUERY_HEADS // KEY_VALUE_HEADS
HEAD_WIDTH = 128
MBLK = 64
VISION_TOKENS = 64
NEGATIVE = -1e30
SCALE = HEAD_WIDTH**-0.5 * 1.4426950408889634

SIDE = 4
ROWS = 128
TEXT = 2 * ROWS
VISION = 2 * VISION_TOKENS
SELF_CHUNKS = 4
SELF_ROWS = 256
CROSS_ROWS = 256


def flat(y, x, z, img):
    return ((y * SIDE + x) * SIDE + z) * 8 + img


def all_places():
    return [
        (y, x, z, img)
        for y in range(SIDE)
        for x in range(SIDE)
        for z in range(SIDE)
        for img in range(8)
    ]


def swap_pairs():
    pairs = []
    for y, x, z, img in all_places():
        core = img % 2
        if core != y // 2:
            pairs.append((flat(y, x, z, img), flat(3 - y, x, z, img ^ 1)))
        else:
            pairs.append((flat(y, x, z, img), flat(y, x, z, img)))
    return pairs


def vision_groups():
    return [
        [flat(yy, x, z, img) for yy in (y, 3 - y) for img in range(8)]
        for y in (0, 1)
        for x in range(SIDE)
        for z in range(SIDE)
    ]


def z_groups():
    return [
        [flat(y, x, z, img) for z in range(SIDE)]
        for y in range(SIDE)
        for x in range(SIDE)
        for img in range(8)
    ]


def plane_groups():
    groups = []
    for half in (0, 1):
        for z in range(SIDE):
            for img in range(8):
                core = img % 2
                held = (0, 1) if core == 0 else (2, 3)
                chips = [h if core == half else 3 - h for h in held]
                groups.append([flat(y, x, z, img) for y in chips for x in range(SIDE)])
    return groups


def scores_of(q, keys, visible):
    scores = lax.dot_general(
        q, keys, (((1,), (1,)), ((), ())), preferred_element_type=jnp.float32
    )
    return scores if visible is None else jnp.where(visible, scores, NEGATIVE)


def mix(scores, shift, values, visible):
    shift = jnp.concatenate([shift] * (scores.shape[1] // 128), axis=1)
    weights = jnp.exp2((scores - shift) * SCALE)
    if visible is not None:
        weights = jnp.where(visible, weights, 0.0)
    both = jnp.concatenate([values, jnp.ones_like(values)], axis=1)
    return jnp.dot(weights.astype(jnp.bfloat16), both, preferred_element_type=jnp.float32)


def first_step(q, keys, values, m_ref, acc_ref, rows, visible):
    scores = scores_of(q, keys, visible)
    top = jnp.broadcast_to(jnp.max(scores, axis=1, keepdims=True), (scores.shape[0], 128))
    m_ref[rows, :] = top
    acc_ref[rows, :] = mix(scores, top, values, visible)


def quick_step(q, keys, values, m_ref, acc_ref, rows, visible):
    scores = scores_of(q, keys, visible)
    acc_ref[rows, :] += mix(scores, m_ref[rows, :], values, visible)


def careful_step(q, keys, values, m_ref, acc_ref, rows, visible):
    scores = scores_of(q, keys, visible)
    old = m_ref[rows, :]
    new = jnp.maximum(old, jnp.max(scores, axis=1, keepdims=True))
    shrink = jnp.exp2((old - new) * SCALE)
    m_ref[rows, :] = new
    acc_ref[rows, :] = acc_ref[rows, :] * jnp.concatenate([shrink, shrink], axis=1) + mix(
        scores, new, values, visible
    )


def steady(acc_ref):
    return jnp.all(acc_ref[:, 128:] < 2.0**100)


def reset(m_ref, acc_ref):
    m_ref[...] = jnp.full_like(m_ref, NEGATIVE)
    acc_ref[...] = jnp.zeros_like(acc_ref)


def cross(meta, core, q_ref, own_ref, other_ref, m_ref, acc_ref, images):
    counts = []
    for b in range(2):
        for part, half in ((0, core), (1, 1 - core)):

            def gather(i, count, b=b, part=part, half=half):
                images[2 * b + part, count] = (i & ~3) | ((meta[0, 65] - i) & 3)
                return count + meta[b, 32 * half + i]

            counts.append(lax.fori_loop(0, 32, gather, 0, unroll=8))

    def load(b, part, start, number):
        ref = (own_ref, other_ref)[part]
        top = jnp.maximum(counts[2 * b + part] - 1, 0)
        picks = [images[2 * b + part, jnp.minimum(start + u, top)] for u in range(number)]
        keys = [ref[i, :VISION_TOKENS, :] for i in picks]
        values = [ref[i, VISION_TOKENS:, :] for i in picks]
        return keys, values

    def run(one_step, b, keys, values, visible):
        keys = jnp.concatenate(keys, axis=0)
        values = jnp.concatenate(values, axis=0)
        for r in range(0, 512, CROSS_ROWS):
            rows = pl.ds(b * 512 + r, CROSS_ROWS)
            one_step(q_ref[rows, :], keys, values, m_ref, acc_ref, rows, visible)

    def sweep(b, begin, later):
        groups = [jnp.maximum(counts[2 * b + part] - 1, 0) // 4 for part in range(2)]
        tails = [counts[2 * b + part] - groups[part] * 4 for part in range(2)]
        keys, values = [], []
        for part in range(2):
            k, v = load(b, part, groups[part] * 4, 4)
            keys += k
            values += v
        width = 4 * VISION_TOKENS
        spot = lax.broadcasted_iota(jnp.int32, (CROSS_ROWS, 2 * width), 1)
        visible = (spot < tails[0] * VISION_TOKENS) | (
            (spot >= width) & (spot < width + tails[1] * VISION_TOKENS)
        )
        run(begin, b, keys, values, visible)
        for part in range(2):
            pairs = groups[part] // 2

            @pl.loop(0, pairs)
            def _(t, part=part):
                run(later, b, *load(b, part, t * 8, 8), None)

            @pl.when(groups[part] % 2 == 1)
            def _(part=part, pairs=pairs):
                run(later, b, *load(b, part, pairs * 8, 4), None)

    for b in range(2):
        sweep(b, first_step, quick_step)

    @pl.when(jnp.logical_not(steady(acc_ref)))
    def _():
        reset(m_ref, acc_ref)
        for b in range(2):
            sweep(b, careful_step, careful_step)


def self_attention(meta, core, q_ref, own_ref, other_ref, m_ref, acc_ref):
    start0 = meta[0, 64] * MBLK
    start1 = meta[1, 64] * MBLK
    row_chunk = meta[0, 65]
    width = SELF_CHUNKS * ROWS
    tiles = 32 // SELF_CHUNKS
    first = start0 // width
    last = row_chunk // SELF_CHUNKS
    clear = (start1 + width - 1) // width

    def tile(one_step, ref, base, t, number, masked):
        keys_wide = number * width
        piece = ref[pl.ds((t - base) * SELF_CHUNKS, number * SELF_CHUNKS), :, :]
        keys = piece[:, :ROWS].reshape(keys_wide, HEAD_WIDTH)
        values = piece[:, ROWS:].reshape(keys_wide, HEAD_WIDTH)
        visible = None
        if masked:
            spot = lax.broadcasted_iota(jnp.int32, (SELF_ROWS, keys_wide), 1)
            spot = t * width + ((row_chunk - spot // ROWS) & 3) * ROWS + spot % ROWS
            row = lax.broadcasted_iota(jnp.int32, (SELF_ROWS, keys_wide), 0) % ROWS
            start = jnp.where(row < MBLK, start0, start1)
            visible = (spot <= row_chunk * ROWS + row) & (spot >= start)
        for r in range(0, GROUP * ROWS, SELF_ROWS):
            rows = pl.ds(r, SELF_ROWS)
            one_step(q_ref[rows, :], keys, values, m_ref, acc_ref, rows, visible)

    def sweep(begin, later):
        tile(begin, own_ref, core * tiles, last, 1, True)
        for ref, half, stop in ((own_ref, core, last), (other_ref, 0, core * tiles)):
            base = half * tiles
            low = jnp.maximum(first, base)
            stop = jnp.maximum(stop, low)
            edge = jnp.clip(clear, low, stop)
            odd = (stop - edge) % 2

            @pl.loop(low, edge)
            def _(t, ref=ref, base=base):
                tile(later, ref, base, t, 1, True)

            @pl.when(odd == 1)
            def _(ref=ref, base=base, edge=edge):
                tile(later, ref, base, edge, 1, False)

            @pl.loop(0, (stop - edge) // 2)
            def _(p, ref=ref, base=base, from_tile=edge + odd):
                tile(later, ref, base, from_tile + 2 * p, 2, False)

    sweep(first_step, quick_step)

    @pl.when(jnp.logical_not(steady(acc_ref)))
    def _():
        reset(m_ref, acc_ref)
        sweep(careful_step, careful_step)


def cross_kernel(meta, q_in, own_ref, other_ref, out_ref, q_ref, m_ref, acc_ref, images):
    places = [(b, g, b * 512 + g * MBLK) for b in range(2) for g in range(GROUP)]
    for b, g, row in places:
        q_ref[row : row + MBLK, :] = q_in[b * MBLK : b * MBLK + MBLK, g * 128 : g * 128 + 128]
    cross(meta, meta[0, 65] // 32, q_ref, own_ref, other_ref, m_ref, acc_ref, images)
    for b, g, row in places:
        rows = slice(row, row + MBLK)
        out_ref[b * MBLK : b * MBLK + MBLK, g * 128 : g * 128 + 128] = (
            acc_ref[rows, :128] / acc_ref[rows, 128:]
        ).astype(jnp.bfloat16)


def self_kernel(meta, q_in, own_ref, other_ref, out_ref, q_ref, m_ref, acc_ref):
    for g in range(GROUP):
        q_ref[g * 128 : g * 128 + 128, :] = q_in[:, g * 128 : g * 128 + 128]
    self_attention(meta, meta[0, 65] // 32, q_ref, own_ref, other_ref, m_ref, acc_ref)
    for g in range(GROUP):
        rows = slice(g * 128, g * 128 + 128)
        out_ref[:, g * 128 : g * 128 + 128] = (acc_ref[rows, :128] / acc_ref[rows, 128:]).astype(
            jnp.bfloat16
        )


def attend(kernel, name, keys, meta, queries, own, other):
    whole = pl.BlockSpec(memory_space=pltpu.VMEM)
    scratch = [
        pltpu.VMEM((GROUP * ROWS, HEAD_WIDTH), jnp.bfloat16),
        pltpu.VMEM((GROUP * ROWS, 128), jnp.float32),
        pltpu.VMEM((GROUP * ROWS, 256), jnp.float32),
    ]
    if kernel is cross_kernel:
        scratch.append(pltpu.SMEM((4, 128), jnp.int32))
    return pl.pallas_call(
        kernel,
        out_shape=jax.ShapeDtypeStruct((ROWS, GROUP * HEAD_WIDTH), jnp.bfloat16),
        in_specs=[pl.BlockSpec(memory_space=pltpu.SMEM), whole, whole, whole],
        out_specs=whole,
        scratch_shapes=scratch,
        compiler_params=pltpu.CompilerParams(vmem_limit_bytes=28 * 1024 * 1024),
        cost_estimate=pl.CostEstimate(
            flops=8 * GROUP * ROWS * keys * HEAD_WIDTH,
            bytes_accessed=4 * keys * HEAD_WIDTH + 4 * GROUP * ROWS * HEAD_WIDTH,
            transcendentals=GROUP * ROWS * keys,
        ),
        name=name,
    )(meta, queries, own, other)


AXES = ("ctx", "img")


def body(self_q, text, cross_q, vision, doc_start, image_mask):
    core = lax.axis_index("img") % 2
    swap = functools.partial(lax.ppermute, axis_name=AXES, perm=swap_pairs())

    with jax.named_scope("text_swap"):
        place = jnp.full((2, 1), lax.axis_index("ctx"), jnp.int32)
        meta = jnp.concatenate([image_mask, (doc_start // MBLK)[:, None], place], axis=1)
        meta = jnp.pad(meta.astype(jnp.bfloat16), ((0, 14), (0, 62)))
        text = jnp.concatenate([text[:, 0], text[:, 1], meta], axis=0)
        heads = vision.reshape(8, 2, 4, 2, HEAD_WIDTH).transpose(3, 2, 1, 0, 4)
        heads = jnp.broadcast_to(heads[:, :, None], (2, 4, 2, 2, 8, HEAD_WIDTH))
        text, heads = lax.optimization_barrier((text, heads))
        text = swap(text)

    def along_z(part):
        pieces = [part]
        for k in range(1, SIDE):
            steps = [
                (flat(y, x, z, img), flat(y, x, (z + k) % SIDE, img)) for y, x, z, img in all_places()
            ]
            pieces.append(lax.ppermute(part, AXES, steps))
        return pieces

    def half_plane(pieces):
        part = jnp.stack(pieces)
        part = jnp.broadcast_to(part[None], (8,) + part.shape)
        part = lax.all_to_all(part, AXES, 0, 0, axis_index_groups=plane_groups(), tiled=True)
        return part.reshape((32,) + part.shape[2:])

    def cores(part):
        return lax.ppermute(part, "img", [(i, i ^ 1) for i in range(8)])

    with jax.named_scope("text_z"):
        text_z = along_z(text[:TEXT])
        meta = text[TEXT : TEXT + 2].astype(jnp.int32)

    with jax.named_scope("vision_heads"):
        heads = lax.all_to_all(
            heads.reshape(16, 16, HEAD_WIDTH), AXES, 0, 0, axis_index_groups=vision_groups(), tiled=True
        )

    with jax.named_scope("query_swap"):
        cross_q = swap(cross_q)
        self_q = swap(self_q)

    text_z, heads, self_q, cross_q = lax.optimization_barrier((text_z, heads, self_q, cross_q))

    with jax.named_scope("vision_z"):
        heads = lax.dynamic_slice_in_dim(heads, core * 8, 8, 0)
        heads = heads.reshape(8, 2, 8, HEAD_WIDTH).transpose(1, 0, 2, 3).reshape(128, HEAD_WIDTH)
        vision_z = along_z(heads)

    with jax.named_scope("text_plane"):
        own_text = half_plane(text_z)

    own_text, vision_z = lax.optimization_barrier((own_text, vision_z))

    with jax.named_scope("vision_plane"):
        own_vision = half_plane(vision_z)

    with jax.named_scope("self_attention"):
        other_text = cores(own_text)
        self_out = attend(self_kernel, "self_attention", 8192, meta, self_q, own_text, other_text)

    self_out, own_vision = lax.optimization_barrier((self_out, own_vision))

    with jax.named_scope("cross_attention"):
        other_vision = cores(own_vision)
        cross_out = attend(
            cross_kernel, "cross_attention", 4096, meta, cross_q, own_vision, other_vision
        )
    return swap(self_out), swap(cross_out)


def solution(mesh):
    placed = (
        P("ctx", "img"),
        P("ctx", None, "img"),
        P("ctx", "img"),
        P("ctx", "img", None, None),
        P("ctx"),
        P("ctx", None),
    )
    return jax.shard_map(
        body,
        mesh=mesh,
        in_specs=placed,
        out_specs=(P("ctx", "img"), P("ctx", "img")),
        check_vma=False,
    )
```

```python
import functools

import jax
import jax.numpy as jnp
from jax import lax
from jax.experimental import pallas as pl
from jax.experimental.pallas import tpu as pltpu
from jax.sharding import PartitionSpec as P

QUERY_HEADS = 64
KEY_VALUE_HEADS = 8
GROUP = QUERY_HEADS // KEY_VALUE_HEADS
HEAD_WIDTH = 128
MBLK = 64
VISION_TOKENS = 64
NEGATIVE = -1e30
SCALE = HEAD_WIDTH**-0.5 * 1.4426950408889634

SIDE = 4
ROWS = 128
TEXT = 2 * ROWS
VISION = 2 * VISION_TOKENS
SELF_CHUNKS = 4
SELF_ROWS = 256
CROSS_ROWS = 256


def flat(y, x, z, img):
    return ((y * SIDE + x) * SIDE + z) * 8 + img


def all_places():
    return [
        (y, x, z, img)
        for y in range(SIDE)
        for x in range(SIDE)
        for z in range(SIDE)
        for img in range(8)
    ]


def swap_pairs():
    pairs = []
    for y, x, z, img in all_places():
        core = img % 2
        if core != y // 2:
            pairs.append((flat(y, x, z, img), flat(3 - y, x, z, img ^ 1)))
        else:
            pairs.append((flat(y, x, z, img), flat(y, x, z, img)))
    return pairs


def vision_groups():
    return [
        [flat(yy, x, z, img) for yy in (y, 3 - y) for img in range(8)]
        for y in (0, 1)
        for x in range(SIDE)
        for z in range(SIDE)
    ]


def z_groups():
    return [
        [flat(y, x, z, img) for z in range(SIDE)]
        for y in range(SIDE)
        for x in range(SIDE)
        for img in range(8)
    ]


def plane_groups():
    groups = []
    for half in (0, 1):
        for z in range(SIDE):
            for img in range(8):
                core = img % 2
                held = (0, 1) if core == 0 else (2, 3)
                chips = [h if core == half else 3 - h for h in held]
                groups.append([flat(y, x, z, img) for y in chips for x in range(SIDE)])
    return groups


def scores_of(q, keys, visible):
    scores = lax.dot_general(
        q, keys, (((1,), (1,)), ((), ())), preferred_element_type=jnp.float32
    )
    return scores if visible is None else jnp.where(visible, scores, NEGATIVE)


def mix(scores, shift, values, visible):
    shift = jnp.concatenate([shift] * (scores.shape[1] // 128), axis=1)
    weights = jnp.exp2((scores - shift) * SCALE)
    if visible is not None:
        weights = jnp.where(visible, weights, 0.0)
    both = jnp.concatenate([values, jnp.ones_like(values)], axis=1)
    return jnp.dot(weights.astype(jnp.bfloat16), both, preferred_element_type=jnp.float32)


def first_step(q, keys, values, m_ref, acc_ref, rows, visible):
    scores = scores_of(q, keys, visible)
    top = jnp.broadcast_to(jnp.max(scores, axis=1, keepdims=True), (scores.shape[0], 128))
    m_ref[rows, :] = top
    acc_ref[rows, :] = mix(scores, top, values, visible)


def quick_step(q, keys, values, m_ref, acc_ref, rows, visible):
    scores = scores_of(q, keys, visible)
    acc_ref[rows, :] += mix(scores, m_ref[rows, :], values, visible)


def careful_step(q, keys, values, m_ref, acc_ref, rows, visible):
    scores = scores_of(q, keys, visible)
    old = m_ref[rows, :]
    new = jnp.maximum(old, jnp.max(scores, axis=1, keepdims=True))
    shrink = jnp.exp2((old - new) * SCALE)
    m_ref[rows, :] = new
    acc_ref[rows, :] = acc_ref[rows, :] * jnp.concatenate([shrink, shrink], axis=1) + mix(
        scores, new, values, visible
    )


def steady(acc_ref):
    return jnp.all(acc_ref[:, 128:] < 2.0**100)


def reset(m_ref, acc_ref):
    m_ref[...] = jnp.full_like(m_ref, NEGATIVE)
    acc_ref[...] = jnp.zeros_like(acc_ref)


def cross(meta, core, q_ref, own_ref, other_ref, m_ref, acc_ref, images):
    counts = []
    for b in range(2):
        for part, half in ((0, core), (1, 1 - core)):

            def gather(i, count, b=b, part=part, half=half):
                images[2 * b + part, count] = i
                return count + meta[b, 32 * half + i]

            counts.append(lax.fori_loop(0, 32, gather, 0, unroll=8))

    def load(b, part, start, number):
        ref = (own_ref, other_ref)[part]
        top = jnp.maximum(counts[2 * b + part] - 1, 0)
        picks = [images[2 * b + part, jnp.minimum(start + u, top)] for u in range(number)]
        keys = [ref[i, :VISION_TOKENS, :] for i in picks]
        values = [ref[i, VISION_TOKENS:, :] for i in picks]
        return keys, values

    def run(one_step, b, keys, values, visible):
        keys = jnp.concatenate(keys, axis=0)
        values = jnp.concatenate(values, axis=0)
        for r in range(0, 512, CROSS_ROWS):
            rows = pl.ds(b * 512 + r, CROSS_ROWS)
            one_step(q_ref[rows, :], keys, values, m_ref, acc_ref, rows, visible)

    def sweep(b, begin, later):
        groups = [jnp.maximum(counts[2 * b + part] - 1, 0) // 4 for part in range(2)]
        tails = [counts[2 * b + part] - groups[part] * 4 for part in range(2)]
        keys, values = [], []
        for part in range(2):
            k, v = load(b, part, groups[part] * 4, 4)
            keys += k
            values += v
        width = 4 * VISION_TOKENS
        spot = lax.broadcasted_iota(jnp.int32, (CROSS_ROWS, 2 * width), 1)
        visible = (spot < tails[0] * VISION_TOKENS) | (
            (spot >= width) & (spot < width + tails[1] * VISION_TOKENS)
        )
        run(begin, b, keys, values, visible)
        for part in range(2):
            pairs = groups[part] // 2

            @pl.loop(0, pairs)
            def _(t, part=part):
                run(later, b, *load(b, part, t * 8, 8), None)

            @pl.when(groups[part] % 2 == 1)
            def _(part=part, pairs=pairs):
                run(later, b, *load(b, part, pairs * 8, 4), None)

    for b in range(2):
        sweep(b, first_step, quick_step)

    @pl.when(jnp.logical_not(steady(acc_ref)))
    def _():
        reset(m_ref, acc_ref)
        for b in range(2):
            sweep(b, careful_step, careful_step)


def self_attention(meta, core, q_ref, own_ref, other_ref, m_ref, acc_ref):
    start0 = meta[0, 64] * MBLK
    start1 = meta[1, 64] * MBLK
    row_chunk = meta[0, 65]
    width = SELF_CHUNKS * ROWS
    tiles = 32 // SELF_CHUNKS
    first = start0 // width
    last = row_chunk // SELF_CHUNKS
    clear = (start1 + width - 1) // width

    def tile(one_step, ref, base, t, number, masked):
        keys_wide = number * width
        piece = ref[pl.ds((t - base) * SELF_CHUNKS, number * SELF_CHUNKS), :, :]
        keys = piece[:, :ROWS].reshape(keys_wide, HEAD_WIDTH)
        values = piece[:, ROWS:].reshape(keys_wide, HEAD_WIDTH)
        visible = None
        if masked:
            spot = t * width + lax.broadcasted_iota(jnp.int32, (SELF_ROWS, keys_wide), 1)
            row = lax.broadcasted_iota(jnp.int32, (SELF_ROWS, keys_wide), 0) % ROWS
            start = jnp.where(row < MBLK, start0, start1)
            visible = (spot <= row_chunk * ROWS + row) & (spot >= start)
        for r in range(0, GROUP * ROWS, SELF_ROWS):
            rows = pl.ds(r, SELF_ROWS)
            one_step(q_ref[rows, :], keys, values, m_ref, acc_ref, rows, visible)

    def sweep(begin, later):
        tile(begin, own_ref, core * tiles, last, 1, True)
        for ref, half, stop in ((own_ref, core, last), (other_ref, 0, core * tiles)):
            base = half * tiles
            low = jnp.maximum(first, base)
            stop = jnp.maximum(stop, low)
            edge = jnp.clip(clear, low, stop)
            odd = (stop - edge) % 2

            @pl.loop(low, edge)
            def _(t, ref=ref, base=base):
                tile(later, ref, base, t, 1, True)

            @pl.when(odd == 1)
            def _(ref=ref, base=base, edge=edge):
                tile(later, ref, base, edge, 1, False)

            @pl.loop(0, (stop - edge) // 2)
            def _(p, ref=ref, base=base, from_tile=edge + odd):
                tile(later, ref, base, from_tile + 2 * p, 2, False)

    sweep(first_step, quick_step)

    @pl.when(jnp.logical_not(steady(acc_ref)))
    def _():
        reset(m_ref, acc_ref)
        sweep(careful_step, careful_step)


def cross_kernel(meta, q_in, own_ref, other_ref, out_ref, q_ref, m_ref, acc_ref, images):
    places = [(b, g, b * 512 + g * MBLK) for b in range(2) for g in range(GROUP)]
    for b, g, row in places:
        q_ref[row : row + MBLK, :] = q_in[
            ROWS + b * MBLK : ROWS + b * MBLK + MBLK, g * 128 : g * 128 + 128
        ]
    cross(meta, meta[0, 65] // 32, q_ref, own_ref, other_ref, m_ref, acc_ref, images)
    for b, g, row in places:
        rows = slice(row, row + MBLK)
        out_ref[b * MBLK : b * MBLK + MBLK, g * 128 : g * 128 + 128] = (
            acc_ref[rows, :128] / acc_ref[rows, 128:]
        ).astype(jnp.bfloat16)


def self_kernel(meta, q_in, own_ref, other_ref, out_ref, q_ref, m_ref, acc_ref):
    for g in range(GROUP):
        q_ref[g * 128 : g * 128 + 128, :] = q_in[:ROWS, g * 128 : g * 128 + 128]
    self_attention(meta, meta[0, 65] // 32, q_ref, own_ref, other_ref, m_ref, acc_ref)
    for g in range(GROUP):
        rows = slice(g * 128, g * 128 + 128)
        out_ref[:, g * 128 : g * 128 + 128] = (acc_ref[rows, :128] / acc_ref[rows, 128:]).astype(
            jnp.bfloat16
        )


def attend(kernel, name, keys, meta, queries, own, other):
    whole = pl.BlockSpec(memory_space=pltpu.VMEM)
    scratch = [
        pltpu.VMEM((GROUP * ROWS, HEAD_WIDTH), jnp.bfloat16),
        pltpu.VMEM((GROUP * ROWS, 128), jnp.float32),
        pltpu.VMEM((GROUP * ROWS, 256), jnp.float32),
    ]
    if kernel is cross_kernel:
        scratch.append(pltpu.SMEM((4, 128), jnp.int32))
    return pl.pallas_call(
        kernel,
        out_shape=jax.ShapeDtypeStruct((ROWS, GROUP * HEAD_WIDTH), jnp.bfloat16),
        in_specs=[pl.BlockSpec(memory_space=pltpu.SMEM), whole, whole, whole],
        out_specs=whole,
        scratch_shapes=scratch,
        compiler_params=pltpu.CompilerParams(vmem_limit_bytes=28 * 1024 * 1024),
        cost_estimate=pl.CostEstimate(
            flops=8 * GROUP * ROWS * keys * HEAD_WIDTH,
            bytes_accessed=4 * keys * HEAD_WIDTH + 4 * GROUP * ROWS * HEAD_WIDTH,
            transcendentals=GROUP * ROWS * keys,
        ),
        name=name,
    )(meta, queries, own, other)


AXES = ("ctx", "img")


def body(self_q, text, cross_q, vision, doc_start, image_mask):
    core = lax.axis_index("img") % 2
    swap = functools.partial(lax.ppermute, axis_name=AXES, perm=swap_pairs())

    with jax.named_scope("text_swap"):
        place = jnp.full((2, 1), lax.axis_index("ctx"), jnp.int32)
        meta = jnp.concatenate([image_mask, (doc_start // MBLK)[:, None], place], axis=1)
        meta = jnp.pad(meta.astype(jnp.bfloat16), ((0, 14), (0, 62)))
        text = jnp.concatenate([text[:, 0], text[:, 1], meta], axis=0)
        text = swap(text)

    def along_z(part):
        part = jnp.broadcast_to(part[None], (SIDE,) + part.shape)
        return lax.all_to_all(part, AXES, 0, 0, axis_index_groups=z_groups(), tiled=True)

    def half_plane(part):
        part = jnp.broadcast_to(part[None], (8,) + part.shape)
        part = lax.all_to_all(part, AXES, 0, 0, axis_index_groups=plane_groups(), tiled=True)
        return part.reshape((32,) + part.shape[2:])

    def cores(part):
        return lax.ppermute(part, "img", [(i, i ^ 1) for i in range(8)])

    with jax.named_scope("vision_heads"):
        heads = vision.reshape(8, 2, 4, 2, HEAD_WIDTH).transpose(3, 2, 1, 0, 4)
        heads = jnp.broadcast_to(heads[:, :, None], (2, 4, 2, 2, 8, HEAD_WIDTH))
        heads = lax.all_to_all(
            heads.reshape(16, 16, HEAD_WIDTH), AXES, 0, 0, axis_index_groups=vision_groups(), tiled=True
        )
        heads = lax.dynamic_slice_in_dim(heads, core * 8, 8, 0)
        heads = heads.reshape(8, 2, 8, HEAD_WIDTH).transpose(1, 0, 2, 3).reshape(128, HEAD_WIDTH)

    with jax.named_scope("query_swap"):
        queries = swap(jnp.concatenate([self_q, cross_q], axis=0))

    text, heads, queries = lax.optimization_barrier((text, heads, queries))
    meta = text[TEXT : TEXT + 2].astype(jnp.int32)

    with jax.named_scope("along_z"):
        piece = along_z(jnp.concatenate([text[:TEXT], heads], axis=0))

    with jax.named_scope("text_plane"):
        own_text = half_plane(piece[:, :TEXT])

    own_text, piece = lax.optimization_barrier((own_text, piece))
    vision_z = piece[:, TEXT:]

    with jax.named_scope("vision_plane"):
        own_vision = half_plane(vision_z)

    with jax.named_scope("self_attention"):
        other_text = cores(own_text)
        self_out = attend(self_kernel, "self_attention", 8192, meta, queries, own_text, other_text)

    self_out, own_vision = lax.optimization_barrier((self_out, own_vision))

    with jax.named_scope("cross_attention"):
        other_vision = cores(own_vision)
        cross_out = attend(
            cross_kernel, "cross_attention", 4096, meta, queries, own_vision, other_vision
        )
    return swap(self_out), swap(cross_out)


def solution(mesh):
    placed = (
        P("ctx", "img"),
        P("ctx", None, "img"),
        P("ctx", "img"),
        P("ctx", "img", None, None),
        P("ctx"),
        P("ctx", None),
    )
    return jax.shard_map(
        body,
        mesh=mesh,
        in_specs=placed,
        out_specs=(P("ctx", "img"), P("ctx", "img")),
        check_vma=False,
    )
```
